1024 devices in a mesh: dp: 128 (over z, y_hi, core), mp: 8 (over x, y_lo).
Axes of the slice: x: 4, y: 8 (y_hi: 4, y_lo: 2; y = y_hi * 2 + y_lo), z: 16, core: 2. Of those that a mesh axis runs over, the one named last changes fastest.
Arguments:
- student_in: bfloat16 [128, 6144], P(None, 'mp'), may hold values from -6 to 6
- teacher_hidden: bfloat16 [8192, 128], P('dp'), may hold values from -6 to 6
- w_up: bfloat16 [24576, 6144], P('dp', 'mp'), may hold values from -0.078125 to 0.078125
- w_down: bfloat16 [24576, 6144], P('dp', 'mp'), may hold values from -0.0390625 to 0.0390625
- w_proj: bfloat16 [8192, 6144], P('dp', 'mp'), may hold values from -0.0625 to 0.0625
Outputs:
- grad_up: float32 [24576, 6144], P('dp', 'mp')
- grad_down: float32 [24576, 6144], P('dp', 'mp')
- grad_proj: float32 [8192, 6144], P('dp', 'mp')
The draws below stay inside these ranges and needn't reach their ends.
All inputs are finite; a program needn't handle non-finite values.
Results may differ from the reference program's by a relative error of at most 0.005.
Values may be sent and summed in bfloat16 or wider, within the bound.
A program may use at most 32 MiB of HBM per device.

```python
import math
import jax
import jax.numpy as jnp

D = 6144
FF = 24576
TD = 8192
TOKENS = 128


def shard_levels(stream_key, dims, shards, least, high):
    factor_of, own = 1.0, jax.random.fold_in(stream_key, 6)
    for axis_at, parts in shards:
        steps = jnp.exp(jax.random.uniform(jax.random.fold_in(own, axis_at), (parts,), jnp.float32, least / len(shards), high / len(shards)))
        factor_of = factor_of * jnp.repeat(steps, dims[axis_at] // parts).reshape([-1 if axis == axis_at else 1 for axis in range(len(dims))])
    return factor_of


def bell_draw(stream_key, dims, width, limit, pieces=(), dtype=jnp.bfloat16):
    loudness = shard_levels(stream_key, dims, pieces, -0.22, 0.18) if pieces else 1.0
    values = jax.random.normal(stream_key, dims, jnp.float32) * width * loudness
    return jnp.minimum(jnp.maximum(values, -limit), limit).astype(dtype)


def setup_inputs(seed: int = 0) -> dict:
    arg_keys = jax.random.split(jax.random.key(seed), 6)
    student_in = bell_draw(arg_keys[0], (TOKENS, D), 1.0, 6.0, ((1, 8),))
    teacher_hidden = bell_draw(arg_keys[1], (TD, TOKENS), 1.0, 6.0, ((0, 128),))
    w_up = bell_draw(arg_keys[2], (FF, D), D ** -0.5, 0.078125, ((0, 128), (1, 8)))
    w_down = bell_draw(arg_keys[3], (FF, D), FF ** -0.5, 0.0390625, ((0, 128), (1, 8)))
    w_proj = bell_draw(arg_keys[4], (TD, D), TD ** -0.5, 0.0625, ((0, 128), (1, 8)))
    return {"student_in": student_in, "teacher_hidden": teacher_hidden, "w_up": w_up, "w_down": w_down, "w_proj": w_proj}


def reference(student_in, teacher_hidden, w_up, w_down, w_proj):
    pre = jnp.dot(w_up, student_in.T, preferred_element_type=jnp.float32)
    active = jnp.maximum(pre, 0.0)
    hidden = (active * active).astype(jnp.bfloat16)
    student_out = jnp.dot(hidden.T, w_down, preferred_element_type=jnp.float32)
    target = jnp.dot(teacher_hidden.T, w_proj, preferred_element_type=jnp.float32)
    residual = student_out - target
    d_out = (residual * (1.0 / math.sqrt(TOKENS))).astype(jnp.bfloat16)
    grad_down = jnp.dot(hidden, d_out, preferred_element_type=jnp.float32)
    grad_proj = -jnp.dot(teacher_hidden, d_out, preferred_element_type=jnp.float32)
    d_hidden = jnp.dot(w_down, d_out.T, preferred_element_type=jnp.float32)
    d_pre = (d_hidden * (2.0 * active)).astype(jnp.bfloat16)
    grad_up = jnp.dot(d_pre, student_in, preferred_element_type=jnp.float32)
    return (grad_up, grad_down, grad_proj)
```

```python
import math

import jax
import jax.numpy as jnp
from jax import lax
from jax.experimental import pallas as pl
from jax.experimental.pallas import tpu as pltpu
from jax.sharding import PartitionSpec as P

F32, BF16 = jnp.float32, jnp.bfloat16
NZ, NY, NC, NX, NL = 16, 4, 2, 4, 2
NM = NX * NL
MESH = pl.DeviceIdType.MESH

WINDOW = [(dz, dy) for dz in (-2, 1, -1, 0) for dy in (2, 1, 3, 0) if dz or dy]
STRIDES = (6, -6, 2, -2)


def nt(a, b):
    return lax.dot_general(a, b, (((1,), (1,)), ((), ())), preferred_element_type=F32)


def tn(a, b):
    return lax.dot_general(a, b, (((0,), (0,)), ((), ())), preferred_element_type=F32)


def nn(a, b):
    return jnp.dot(a, b, preferred_element_type=F32)


def step_kernel(
    x_h, th_h, wu_h, wd_h, wp_h,
    gu_h, gd_h, gp_h,
    x, th, wu, wd, wp, gu, gd, gp,
    pre_s, pre_r, act, hid, ht, ht2, tgt, tgt_r,
    res_s, res_r, win, far_r, piece, dfull, dh_s, dh_r, dpt,
    in_sem, out_sem, core_ss, core_rs,
    a1_ss, a1_rs, a2_ss, a2_rs, b1_ss, b1_rs, b2_ss, b2_rs, c_ss, c_rs, d1_ss, d1_rs, d2_ss, d2_rs,
):
    ff = wu.shape[0]
    half = x.shape[0] // 2
    cols = piece.shape[1]
    dp, mp = lax.axis_index("dp"), lax.axis_index("mp")
    z, y, c = dp // (NY * NC), (dp // NC) % NY, dp % NC
    oc = 1 - c
    own_half = mp // (NM // 2)
    tok = mp % (NM // 2)

    def at(dz, dy):
        return lax.rem(z + dz + NZ, NZ), lax.rem(y + dy + NY, NY)

    def device(zz, yy, cc, mm):
        return (zz * (NY * NC) + yy * NC + cc, mm)

    barrier = pltpu.get_barrier_semaphore()
    senders = [(-s, 0) for s in STRIDES if (s, 0) not in WINDOW] + [(-dz, -dy) for dz, dy in WINDOW]
    for dz, dy in senders:
        zz, yy = at(dz, dy)
        pl.semaphore_signal(barrier, inc=1, device_id=device(zz, yy, c, mp), device_id_type=MESH)
    for dc in range(NC):
        for dm in range(NM):
            if dc or dm:
                cc, mm = lax.rem(c + dc, NC), lax.rem(mp + dm, NM)
                pl.semaphore_signal(barrier, inc=1, device_id=device(z, y, cc, mm), device_id_type=MESH)

    loads = [
        pltpu.make_async_copy(src, dst, in_sem.at[i])
        for i, (src, dst) in enumerate(((x_h, x), (wu_h, wu), (th_h, th), (wp_h, wp), (wd_h, wd.at[c])))
    ]
    for load in loads:
        load.start()
    sent = []

    def send(src, dst, ss, rs, dev):
        copy = pltpu.make_async_remote_copy(
            src_ref=src, dst_ref=dst, send_sem=ss, recv_sem=rs, device_id=dev, device_id_type=MESH
        )
        copy.start()
        sent.append(copy)

    def arrived(dst, sem):
        pltpu.make_async_copy(dst, dst, sem).wait()

    loads[0].wait()
    loads[1].wait()
    part = nt(x[...], wu[...])
    for m in range(NM):
        pre_s[m, :, :ff] = part[16 * m : 16 * m + 16]
    pl.semaphore_wait(barrier, len(senders) + NC * NM - 1)
    for d in range(1, NM):
        mm = lax.rem(mp + d, NM)
        send(pre_s.at[mm], pre_r.at[mp], a1_ss.at[d], a1_rs.at[mp], device(z, y, c, mm))
    partner = device(z, y, oc, mp)
    send(wd_h, wd.at[c], core_ss.at[0], core_rs.at[0], partner)

    loads[2].wait()
    loads[3].wait()
    goal = tn(th[...], wp[...])
    for i in range(NC):
        tgt[i] = goal[half * i : half * i + half]
    send(tgt.at[oc], tgt_r, core_ss.at[1], core_rs.at[1], partner)

    total = pre_s[mp]
    for d in range(1, NM):
        mm = lax.rem(mp + d, NM)
        arrived(pre_r.at[mm], a1_rs.at[mm])
        total = total + pre_r[mm]
    active = jnp.maximum(total, 0.0)
    hid[...] = (active * active).astype(BF16)
    for d in range(1, NM):
        mm = lax.rem(mp + d, NM)
        send(hid, ht.at[c, tok], a2_ss.at[d], a2_rs.at[c * (NM // 2) + tok], device(z, y, own_half, mm))
    keep = pltpu.make_async_copy(hid, ht.at[c, tok], a2_rs.at[c * (NM // 2) + tok])
    give = pltpu.make_async_remote_copy(
        src_ref=hid, dst_ref=ht.at[c, tok], send_sem=a2_ss.at[0], recv_sem=a2_rs.at[c * (NM // 2) + tok],
        device_id=partner, device_id_type=MESH,
    )

    @pl.when(own_half == c)
    def _():
        keep.start()

    @pl.when(own_half != c)
    def _():
        give.start()

    act[...] = 2.0 * active
    loads[4].wait()
    arrived(wd.at[oc], core_rs.at[0])
    arrived(tgt_r, core_rs.at[1])
    base = tgt[c] + tgt_r[...]
    for i in range(NC):
        for t in range(NM // 2):
            arrived(ht.at[i, t], a2_rs.at[i * (NM // 2) + t])

    part = -base
    for i in range(NC):
        part = part + nn(ht[i].reshape(half, ht.shape[-1])[:, :ff], wd[i])
    groups = half // 8
    for h in range(2):
        res_s[groups * h : groups * h + groups] = part[:, cols * h : cols * h + cols].reshape(groups, 8, cols)
    for j, (dz, dy) in enumerate(WINDOW):
        zz, yy = at(dz, dy)
        send(res_s.at[yy * 4 + lax.rem(zz, 4)], res_r.at[j], b1_ss.at[j], b1_rs.at[j], device(zz, yy, c, mp))
    send(ht.at[oc], ht2, core_ss.at[2], core_rs.at[2], partner)
    total = res_s[y * 4 + lax.rem(z, 4)]
    for j in reversed(range(len(WINDOW))):
        arrived(res_r.at[j], b1_rs.at[j])
        total = total + res_r[j]
    win[...] = total
    for j, s in enumerate(STRIDES):
        zz, yy = at(s, 0)
        send(win, far_r.at[j], b2_ss.at[j], b2_rs.at[j], device(zz, yy, c, mp))
    for j in range(len(STRIDES)):
        arrived(far_r.at[j], b2_rs.at[j])
    residual = (far_r[0] + far_r[1]) + (far_r[2] + far_r[3])
    piece[...] = (residual * (1.0 / math.sqrt(2 * half))).astype(BF16)
    mine = y * 4 + lax.rem(z + 2, 4)
    for j, (dz, dy) in enumerate(WINDOW):
        zz, yy = at(dz, dy)
        send(piece, dfull.at[c, mine], c_ss.at[j], c_rs.at[j], device(zz, yy, c, mp))
    dfull[c, mine] = piece[...]
    for j, (dz, dy) in enumerate(WINDOW):
        zz, yy = at(-dz, -dy)
        arrived(dfull.at[c, yy * 4 + lax.rem(zz + 2, 4)], c_rs.at[j])
    send(dfull.at[c], dfull.at[c], core_ss.at[3], core_rs.at[3], partner)

    def d_half(i, h):
        return dfull[i, groups * h : groups * h + groups].reshape(half, cols)

    d_own = [d_half(c, h) for h in range(2)]
    for i in range(NC):
        part = nt(d_own[0], wd[i, :, :cols]) + nt(d_own[1], wd[i, :, cols:])
        dh_s[i, :, :, :ff] = part.reshape(NM // 2, 16, ff)
    for e in range(NC):
        for d in range(NM // 2):
            if e or d:
                i, t = lax.rem(c + e, NC), lax.rem(tok + d, NM // 2)
                k = e * (NM // 2) + d
                send(dh_s.at[i, t], dh_r.at[mp], d1_ss.at[k], d1_rs.at[mp], device(z, y, i, c * (NM // 2) + t))
    keep2 = pltpu.make_async_copy(dh_s.at[c, tok], dh_r.at[mp], d1_rs.at[mp])
    give2 = pltpu.make_async_remote_copy(
        src_ref=dh_s.at[c, tok], dst_ref=dh_r.at[mp], send_sem=d1_ss.at[0], recv_sem=d1_rs.at[mp],
        device_id=device(z, y, c, c * (NM // 2) + tok), device_id_type=MESH,
    )

    @pl.when(own_half == c)
    def _():
        keep2.start()

    @pl.when(own_half != c)
    def _():
        give2.start()

    arrived(dfull.at[oc], core_rs.at[3])
    arrived(ht2, core_rs.at[2])
    d_other = [d_half(oc, h) for h in range(2)]
    h_own = ht[c].reshape(half, ht.shape[-1])[:, :ff]
    h_other = ht2[...].reshape(half, ht.shape[-1])[:, :ff]
    d_nat = [[d_half(i, h) for h in range(2)] for i in range(NC)]
    for h in range(2):
        gd[:, cols * h : cols * h + cols] = tn(h_own, d_own[h]) + tn(h_other, d_other[h])
        gp[:, cols * h : cols * h + cols] = -(nn(th[:, :half], d_nat[0][h]) + nn(th[:, half:], d_nat[1][h]))
    outs = [
        pltpu.make_async_copy(src, dst, out_sem.at[i])
        for i, (src, dst) in enumerate(((gd, gd_h), (gp, gp_h), (gu, gu_h)))
    ]
    outs[0].start()
    outs[1].start()

    for m in range(NM):
        arrived(dh_r.at[m], d1_rs.at[m])
    total = dh_r[0]
    for m in range(1, NM):
        total = total + dh_r[m]
    dpt[mp] = (total * act[...]).astype(BF16)
    for d in range(1, NM):
        mm = lax.rem(mp + d, NM)
        send(dpt.at[mp], dpt.at[mp], d2_ss.at[d], d2_rs.at[mp], device(z, y, c, mm))
    for d in range(1, NM):
        mm = lax.rem(mp + d, NM)
        arrived(dpt.at[mm], d2_rs.at[mm])
    gu[...] = tn(dpt[...].reshape(2 * half, dpt.shape[-1])[:, :ff], x[...])
    outs[2].start()
    for copy in sent:
        copy.wait_send()

    @pl.when(own_half != c)
    def _():
        give.wait_send()
        give2.wait_send()

    for out in outs:
        out.wait()


def body(student_in, teacher_hidden, w_up, w_down, w_proj):
    tokens, width = student_in.shape
    ff, td = w_up.shape[0], w_proj.shape[0]
    half, cols = tokens // 2, width // 2
    wide = 256
    any_ = pl.BlockSpec(memory_space=pl.ANY)
    sem = pltpu.SemaphoreType.DMA
    vm = pltpu.VMEM
    scratch = [
        vm((tokens, width), BF16), vm((td, tokens), BF16), vm((ff, width), BF16), vm((NC, ff, width), BF16),
        vm((td, width), BF16), vm((ff, width), F32), vm((ff, width), F32), vm((td, width), F32),
        vm((NM, 16, wide), F32), vm((NM, 16, wide), F32), vm((16, wide), F32), vm((16, wide), BF16),
        vm((NC, NM // 2, 16, wide), BF16), vm((NM // 2, 16, wide), BF16),
        vm((NC, half, width), F32), vm((half, width), F32),
        vm((16, 8, cols), F32), vm((15, 8, cols), F32), vm((8, cols), F32), vm((4, 8, cols), F32),
        vm((8, cols), BF16), vm((NC, 16, 8, cols), BF16),
        vm((NC, NM // 2, 16, wide), F32), vm((NM, 16, wide), F32), vm((NM, 16, wide), BF16),
        sem((5,)), sem((3,)), sem((4,)), sem((4,)),
        sem((8,)), sem((8,)), sem((8,)), sem((8,)), sem((15,)), sem((15,)), sem((4,)), sem((4,)),
        sem((15,)), sem((15,)), sem((8,)), sem((8,)), sem((8,)), sem((8,)),
    ]
    return pl.pallas_call(
        step_kernel,
        out_shape=(
            jax.ShapeDtypeStruct((ff, width), F32),
            jax.ShapeDtypeStruct((ff, width), F32),
            jax.ShapeDtypeStruct((td, width), F32),
        ),
        in_specs=[any_] * 5,
        out_specs=(any_,) * 3,
        scratch_shapes=scratch,
        compiler_params=pltpu.CompilerParams(
            collective_id=0, has_side_effects=True, vmem_limit_bytes=40 * 1024 * 1024
        ),
        name="distill_step",
    )(student_in, teacher_hidden, w_up, w_down, w_proj)


def solution(mesh):
    return jax.shard_map(
        body,
        mesh=mesh,
        in_specs=(P(None, "mp"), P("dp", None), P("dp", "mp"), P("dp", "mp"), P("dp", "mp")),
        out_specs=(P("dp", "mp"), P("dp", "mp"), P("dp", "mp")),
        check_vma=False,
    )
```

```python
import math

import jax
import jax.numpy as jnp
from jax import lax
from jax.experimental import pallas as pl
from jax.experimental.pallas import tpu as pltpu
from jax.sharding import PartitionSpec as P

F32, BF16 = jnp.float32, jnp.bfloat16
NZ, NY, NC, NX, NL = 16, 4, 2, 4, 2
NM = NX * NL
MESH = pl.DeviceIdType.MESH

WINDOW = (
    (0, 2), (2, 1), (2, -1), (3, 0), (-3, 0), (1, 1), (1, -1), (-1, 1), (-1, -1),
    (2, 0), (-2, 0), (0, 1), (0, -1), (1, 0), (-1, 0),
)
FAR = ((8, 0), (4, 2), (-4, 2))
MP_ORDER = (5, 3, 4, 2, 6, 7, 1)


def nt(a, b):
    return lax.dot_general(a, b, (((1,), (1,)), ((), ())), preferred_element_type=F32)


def tn(a, b):
    return lax.dot_general(a, b, (((0,), (0,)), ((), ())), preferred_element_type=F32)


def nn(a, b):
    return jnp.dot(a, b, preferred_element_type=F32)


def step_kernel(
    x_h, th_h, wu_h, wd_h, wp_h,
    x, dpt, gd, gp,
    th, wu, wd, wp,
    pre_s, pre_r, act, hid, ht, ht2, tgt, tgt_r,
    res_s, res_r, win, far_r, piece, dfull, dh_s, dh_r,
    go, in_sem, core_ss, core_rs,
    a1_ss, a1_rs, a2_ss, a2_rs, b1_ss, b1_rs, b2_ss, b2_rs, c_ss, c_rs, d1_ss, d1_rs, d2_ss, d2_rs,
):
    ff = wu.shape[0]
    half = x.shape[0] // 2
    cols = piece.shape[1]
    quarter = NM // 2
    dp, mp = lax.axis_index("dp"), lax.axis_index("mp")
    z, y, c = dp // (NY * NC), (dp // NC) % NY, dp % NC
    oc = 1 - c
    mirror = 1 - 2 * c
    own_half = mp // quarter
    tok = mp % quarter

    loads = [
        pltpu.make_async_copy(src, dst, in_sem.at[i])
        for i, (src, dst) in enumerate(((x_h, x), (wu_h, wu), (th_h, th), (wp_h, wp), (wd_h, wd.at[c])))
    ]
    loads[0].start()
    loads[1].start()

    def at(dz, dy, sign=1):
        return lax.rem(z + sign * mirror * dz + NZ, NZ), lax.rem(y + sign * dy + NY, NY)

    def device(zz, yy, cc, mm):
        return (zz * (NY * NC) + yy * NC + cc, mm)

    def owned(zz, yy):
        return lax.rem(yy + 2 * (zz // 4), NY) * 4 + lax.rem(zz, 4)

    def signal(sem, dev):
        pl.semaphore_signal(sem, inc=1, device_id=dev, device_id_type=MESH)

    partner = device(z, y, oc, mp)
    barrier = pltpu.get_barrier_semaphore()
    for d in MP_ORDER:
        signal(barrier, device(z, y, 0, lax.rem(mp + d, NM)))

    @pl.when(c == 1)
    def _():
        signal(barrier, partner)

    for dz, dy in FAR + WINDOW:
        zz, yy = at(dz, dy, -1)
        signal(barrier, device(zz, yy, 1, mp))
    for load in loads[2:]:
        load.start()

    def send(src, dst, ss, rs, dev):
        copy = pltpu.make_async_remote_copy(
            src_ref=src, dst_ref=dst, send_sem=ss, recv_sem=rs, device_id=dev, device_id_type=MESH
        )
        copy.start()
        return copy

    def arrived(dst, sem):
        pltpu.make_async_copy(dst, dst, sem).wait()

    def left(copies):
        for copy in copies:
            copy.wait_send()

    loads[0].wait()
    loads[1].wait()
    part = nt(x[...], wu[...])
    for m in range(NM):
        pre_s[m, :, :ff] = part[16 * m : 16 * m + 16]

    @pl.when(c == 0)
    def _():
        pl.semaphore_wait(barrier, NC * NM - 1)
        signal(go, partner)

    @pl.when(c == 1)
    def _():
        pl.semaphore_wait(go, 1)

    sent = []
    for d in MP_ORDER:
        mm = lax.rem(mp + d, NM)
        sent.append(send(pre_s.at[mm], pre_r.at[mp], a1_ss.at[d], a1_rs.at[mp], device(z, y, c, mm)))
    loads[4].wait()
    sent.append(send(wd.at[c], wd.at[c], core_ss.at[0], core_rs.at[0], partner))

    loads[2].wait()
    loads[3].wait()
    goal = tn(th[...], wp[...])
    for i in range(NC):
        tgt[i] = goal[half * i : half * i + half]
    sent.append(send(tgt.at[oc], tgt_r, core_ss.at[1], core_rs.at[1], partner))

    total = pre_s[mp]
    for d in reversed(MP_ORDER):
        mm = lax.rem(mp + d, NM)
        arrived(pre_r.at[mm], a1_rs.at[mm])
        total = total + pre_r[mm]
    active = jnp.maximum(total, 0.0)
    hid[...] = (active * active).astype(BF16)
    slot = c * quarter + tok
    for d in MP_ORDER:
        mm = lax.rem(mp + d, NM)
        sent.append(send(hid, ht.at[c, tok], a2_ss.at[d], a2_rs.at[slot], device(z, y, own_half, mm)))
    keep = pltpu.make_async_copy(hid, ht.at[c, tok], a2_rs.at[slot])
    give = pltpu.make_async_remote_copy(
        src_ref=hid, dst_ref=ht.at[c, tok], send_sem=a2_ss.at[0], recv_sem=a2_rs.at[slot],
        device_id=partner, device_id_type=MESH,
    )

    @pl.when(own_half == c)
    def _():
        keep.start()

    @pl.when(own_half != c)
    def _():
        give.start()

    act[...] = 2.0 * active

    @pl.when(c == 1)
    def _():
        pl.semaphore_wait(barrier, NC * (len(FAR) + len(WINDOW)))
        signal(go, partner)

    @pl.when(c == 0)
    def _():
        pl.semaphore_wait(go, 1)

    arrived(wd.at[oc], core_rs.at[0])
    arrived(tgt_r, core_rs.at[1])
    base = tgt[c] + tgt_r[...]
    for i in range(NC):
        for t in range(quarter):
            arrived(ht.at[i, t], a2_rs.at[i * quarter + t])

    part = -base
    for i in range(NC):
        part = part + nn(ht[i].reshape(half, ht.shape[-1])[:, :ff], wd[i])
    groups = half // 8
    for h in range(2):
        res_s[groups * h : groups * h + groups] = part[:, cols * h : cols * h + cols].reshape(groups, 8, cols)
    sent_b = []
    for j, (dz, dy) in enumerate(WINDOW):
        zz, yy = at(dz, dy)
        sent_b.append(send(res_s.at[owned(zz, yy)], res_r.at[j], b1_ss.at[j], b1_rs.at[j], device(zz, yy, c, mp)))
    sent.append(send(ht.at[oc], ht2, core_ss.at[2], core_rs.at[2], partner))
    left(sent)

    @pl.when(own_half != c)
    def _():
        give.wait_send()

    mine = owned(z, y)
    total = res_s[mine]
    for j in reversed(range(len(WINDOW))):
        arrived(res_r.at[j], b1_rs.at[j])
        total = total + res_r[j]
    win[...] = total
    for j, (dz, dy) in enumerate(FAR):
        zz, yy = at(dz, dy)
        sent_b.append(send(win, far_r.at[j], b2_ss.at[j], b2_rs.at[j], device(zz, yy, c, mp)))
    left(sent_b[: len(WINDOW)])
    residual = total
    for j in range(len(FAR)):
        arrived(far_r.at[j], b2_rs.at[j])
        residual = residual + far_r[j]
    piece[...] = (residual * (1.0 / math.sqrt(2 * half))).astype(BF16)
    sent = []
    for j, (dz, dy) in enumerate(WINDOW):
        zz, yy = at(dz, dy)
        sent.append(send(piece, dfull.at[c, mine], c_ss.at[j], c_rs.at[j], device(zz, yy, c, mp)))
    dfull[c, mine] = piece[...]
    left(sent_b[len(WINDOW) :])
    for j, (dz, dy) in enumerate(WINDOW):
        zz, yy = at(dz, dy, -1)
        arrived(dfull.at[c, owned(zz, yy)], c_rs.at[j])

    def d_half(i, h):
        return dfull[i, groups * h : groups * h + groups].reshape(half, cols)

    d_own = [d_half(c, h) for h in range(2)]
    sent_d = []
    for e in (1, 0):
        i = lax.rem(c + e, NC)
        part = nt(d_own[0], wd[i, :, :cols]) + nt(d_own[1], wd[i, :, cols:])
        dh_s[i, :, :, :ff] = part.reshape(quarter, 16, ff)
        for d in (2, 1, 3, 0):
            if e or d:
                t = lax.rem(tok + d, quarter)
                dev = device(z, y, i, c * quarter + t)
                sent_d.append(send(dh_s.at[i, t], dh_r.at[mp], d1_ss.at[e * quarter + d], d1_rs.at[mp], dev))
    keep2 = pltpu.make_async_copy(dh_s.at[c, tok], dh_r.at[mp], d1_rs.at[mp])
    give2 = pltpu.make_async_remote_copy(
        src_ref=dh_s.at[c, tok], dst_ref=dh_r.at[mp], send_sem=d1_ss.at[0], recv_sem=d1_rs.at[mp],
        device_id=device(z, y, c, c * quarter + tok), device_id_type=MESH,
    )

    @pl.when(own_half == c)
    def _():
        keep2.start()

    @pl.when(own_half != c)
    def _():
        give2.start()

    sent.append(send(dfull.at[c], dfull.at[c], core_ss.at[3], core_rs.at[3], partner))
    left(sent)
    total = None
    for m in range(NM):
        arrived(dh_r.at[m], d1_rs.at[m])
        total = dh_r[m] if total is None else total + dh_r[m]
    dpt[mp] = (total * act[...]).astype(BF16)
    sent = []
    for d in MP_ORDER:
        mm = lax.rem(mp + d, NM)
        sent.append(send(dpt.at[mp], dpt.at[mp], d2_ss.at[d], d2_rs.at[mp], device(z, y, c, mm)))

    left(sent_d)

    @pl.when(own_half != c)
    def _():
        give2.wait_send()

    arrived(dfull.at[oc], core_rs.at[3])
    arrived(ht2, core_rs.at[2])
    h_own = ht[c].reshape(half, ht.shape[-1])[:, :ff]
    h_other = ht2[...].reshape(half, ht.shape[-1])[:, :ff]
    for h in range(2):
        d_nat = [d_half(i, h) for i in range(NC)]
        gd[:, cols * h : cols * h + cols] = tn(h_own, d_half(c, h)) + tn(h_other, d_half(oc, h))
        gp[:, cols * h : cols * h + cols] = -(nn(th[:, :half], d_nat[0]) + nn(th[:, half:], d_nat[1]))

    for d in MP_ORDER:
        mm = lax.rem(mp + d, NM)
        arrived(dpt.at[mm], d2_rs.at[mm])
    left(sent)


def last_kernel(dpt, x, gd, gp, gu_h, gd_h, gp_h, gu, sem):
    ff = gu.shape[0]
    done = [pltpu.make_async_copy(gd, gd_h, sem.at[0]), pltpu.make_async_copy(gp, gp_h, sem.at[1])]
    for copy in done:
        copy.start()
    rows = dpt[...].reshape(x.shape[0], dpt.shape[-1])[:, :ff]
    step = x.shape[1] // 3
    for i in range(3):
        gu[:, step * i : step * i + step] = tn(rows, x[:, step * i : step * i + step])
        copy = pltpu.make_async_copy(
            gu.at[:, pl.ds(step * i, step)], gu_h.at[:, pl.ds(step * i, step)], sem.at[2 + i]
        )
        copy.start()
        done.append(copy)
    for copy in done:
        copy.wait()


def body(student_in, teacher_hidden, w_up, w_down, w_proj):
    tokens, width = student_in.shape
    ff, td = w_up.shape[0], w_proj.shape[0]
    half, cols = tokens // 2, width // 2
    wide = 256
    hbm, vmem = pl.BlockSpec(memory_space=pltpu.HBM), pl.BlockSpec(memory_space=pltpu.VMEM)
    any_ = pl.BlockSpec(memory_space=pl.ANY)
    sem = pltpu.SemaphoreType.DMA
    vm = pltpu.VMEM
    scratch = [
        vm((td, tokens), BF16), vm((ff, width), BF16), vm((NC, ff, width), BF16),
        vm((td, width), BF16),
        vm((NM, 16, wide), F32), vm((NM, 16, wide), F32), vm((16, wide), F32), vm((16, wide), BF16),
        vm((NC, NM // 2, 16, wide), BF16), vm((NM // 2, 16, wide), BF16),
        vm((NC, half, width), F32), vm((half, width), F32),
        vm((16, 8, cols), F32), vm((15, 8, cols), F32), vm((8, cols), F32), vm((3, 8, cols), F32),
        vm((8, cols), BF16), vm((NC, 16, 8, cols), BF16),
        vm((NC, NM // 2, 16, wide), F32), vm((NM, 16, wide), F32),
        pltpu.SemaphoreType.REGULAR, sem((5,)), sem((4,)), sem((4,)),
        sem((8,)), sem((8,)), sem((8,)), sem((8,)), sem((15,)), sem((15,)), sem((3,)), sem((3,)),
        sem((15,)), sem((15,)), sem((8,)), sem((8,)), sem((8,)), sem((8,)),
    ]
    grads = [jax.ShapeDtypeStruct((rows, width), F32) for rows in (ff, ff, td)]
    x, dpt, gd, gp = pl.pallas_call(
        step_kernel,
        out_shape=(
            jax.ShapeDtypeStruct((tokens, width), BF16),
            jax.ShapeDtypeStruct((NM, 16, wide), BF16),
            *grads[1:],
        ),
        in_specs=[hbm] * 5,
        out_specs=(vmem,) * 4,
        scratch_shapes=scratch,
        compiler_params=pltpu.CompilerParams(
            collective_id=0, has_side_effects=True, vmem_limit_bytes=40 * 1024 * 1024
        ),
        name="distill_step",
    )(*(pltpu.with_memory_space_constraint(a, pltpu.HBM) for a in (student_in, teacher_hidden, w_up, w_down, w_proj)))
    return pl.pallas_call(
        last_kernel,
        out_shape=tuple(grads),
        in_specs=[vmem, vmem, any_, any_],
        out_specs=(any_,) * 3,
        scratch_shapes=[vm((ff, width), F32), sem((5,))],
        compiler_params=pltpu.CompilerParams(vmem_limit_bytes=4 * 1024 * 1024),
        name="grad_up",
    )(dpt, x, gd, gp)


def solution(mesh):
    return jax.shard_map(
        body,
        mesh=mesh,
        in_specs=(P(None, "mp"), P("dp", None), P("dp", "mp"), P("dp", "mp"), P("dp", "mp")),
        out_specs=(P("dp", "mp"), P("dp", "mp"), P("dp", "mp")),
        check_vma=False,
    )
```

```python
import math

import jax
import jax.numpy as jnp
from jax import lax
from jax.experimental import pallas as pl
from jax.experimental.pallas import tpu as pltpu
from jax.sharding import PartitionSpec as P

F32, BF16 = jnp.float32, jnp.bfloat16
NZ, NY, NC, NX, NL = 16, 4, 2, 4, 2
NM = NX * NL
MESH = pl.DeviceIdType.MESH

WINDOW = (
    (0, 2), (2, 1), (2, -1), (3, 0), (-3, 0), (1, 1), (1, -1), (-1, 1), (-1, -1),
    (2, 0), (-2, 0), (0, 1), (0, -1), (1, 0), (-1, 0),
)
FAR = ((8, 0), (4, 2), (-4, 2))
MP_ORDER = (5, 3, 4, 2, 6, 7, 1)


def nt(a, b):
    return lax.dot_general(a, b, (((1,), (1,)), ((), ())), preferred_element_type=F32)


def tn(a, b):
    return lax.dot_general(a, b, (((0,), (0,)), ((), ())), preferred_element_type=F32)


def nn(a, b):
    return jnp.dot(a, b, preferred_element_type=F32)


def step_kernel(
    x_h, th_h, wu_h, wd_h, wp_h,
    x, dpt, gd, gp,
    th, wu, wd, wp,
    pre_s, pre_r, act, hid, ht, ht2, tgt, tgt_r,
    res_s, res_r, win, far_r, piece, dfull, dh_s, dh_f, dh_p, dh_r,
    go, in_sem, core_ss, core_rs,
    a1_ss, a1_rs, a2_ss, a2_rs, b1_ss, b1_rs, b2_ss, b2_rs, c_ss, c_rs, d1_ss, d1_rs, act_ss, act_rs,
):
    ff = wu.shape[0]
    half = x.shape[0] // 2
    cols = piece.shape[1]
    quarter = NM // 2
    dp, mp = lax.axis_index("dp"), lax.axis_index("mp")
    z, y, c = dp // (NY * NC), (dp // NC) % NY, dp % NC
    oc = 1 - c
    mirror = 1 - 2 * c
    own_half = mp // quarter
    tok = mp % quarter

    loads = [
        pltpu.make_async_copy(src, dst, in_sem.at[i])
        for i, (src, dst) in enumerate(((x_h, x), (wu_h, wu), (th_h, th), (wp_h, wp), (wd_h, wd.at[c])))
    ]
    loads[0].start()
    loads[1].start()

    def at(dz, dy, sign=1):
        return lax.rem(z + sign * mirror * dz + NZ, NZ), lax.rem(y + sign * dy + NY, NY)

    def device(zz, yy, cc, mm):
        return (zz * (NY * NC) + yy * NC + cc, mm)

    def owned(zz, yy):
        return lax.rem(yy + 2 * (zz // 4), NY) * 4 + lax.rem(zz, 4)

    def signal(sem, dev):
        pl.semaphore_signal(sem, inc=1, device_id=dev, device_id_type=MESH)

    partner = device(z, y, oc, mp)
    barrier = pltpu.get_barrier_semaphore()
    for d in MP_ORDER:
        signal(barrier, device(z, y, 0, lax.rem(mp + d, NM)))

    @pl.when(c == 1)
    def _():
        signal(barrier, partner)

    for dz, dy in FAR + WINDOW:
        zz, yy = at(dz, dy, -1)
        signal(barrier, device(zz, yy, 1, mp))
    for load in loads[2:]:
        load.start()

    def send(src, dst, ss, rs, dev):
        copy = pltpu.make_async_remote_copy(
            src_ref=src, dst_ref=dst, send_sem=ss, recv_sem=rs, device_id=dev, device_id_type=MESH
        )
        copy.start()
        return copy

    def arrived(dst, sem):
        pltpu.make_async_copy(dst, dst, sem).wait()

    def left(copies):
        for copy in copies:
            copy.wait_send()

    loads[0].wait()
    loads[1].wait()
    part = nt(x[...], wu[...])
    for m in range(NM):
        pre_s[m, :, :ff] = part[16 * m : 16 * m + 16]

    @pl.when(c == 0)
    def _():
        pl.semaphore_wait(barrier, NC * NM - 1)
        signal(go, partner)

    @pl.when(c == 1)
    def _():
        pl.semaphore_wait(go, 1)

    sent = []
    for d in MP_ORDER:
        mm = lax.rem(mp + d, NM)
        sent.append(send(pre_s.at[mm], pre_r.at[mp], a1_ss.at[d], a1_rs.at[mp], device(z, y, c, mm)))
    loads[4].wait()
    sent.append(send(wd.at[c], wd.at[c], core_ss.at[0], core_rs.at[0], partner))

    loads[2].wait()
    loads[3].wait()
    goal = tn(th[...], wp[...])
    for i in range(NC):
        tgt[i] = goal[half * i : half * i + half]
    sent.append(send(tgt.at[oc], tgt_r, core_ss.at[1], core_rs.at[1], partner))

    total = pre_s[mp]
    for d in reversed(MP_ORDER):
        mm = lax.rem(mp + d, NM)
        arrived(pre_r.at[mm], a1_rs.at[mm])
        total = total + pre_r[mm]
    active = jnp.maximum(total, 0.0)
    hid[...] = (active * active).astype(BF16)
    slot = c * quarter + tok
    for d in MP_ORDER:
        mm = lax.rem(mp + d, NM)
        sent.append(send(hid, ht.at[c, tok], a2_ss.at[d], a2_rs.at[slot], device(z, y, own_half, mm)))
    keep = pltpu.make_async_copy(hid, ht.at[c, tok], a2_rs.at[slot])
    give = pltpu.make_async_remote_copy(
        src_ref=hid, dst_ref=ht.at[c, tok], send_sem=a2_ss.at[0], recv_sem=a2_rs.at[slot],
        device_id=partner, device_id_type=MESH,
    )

    @pl.when(own_half == c)
    def _():
        keep.start()

    @pl.when(own_half != c)
    def _():
        give.start()

    act[mp] = 2.0 * active

    @pl.when(c == 1)
    def _():
        pl.semaphore_wait(barrier, NC * (len(FAR) + len(WINDOW)))
        signal(go, partner)

    @pl.when(c == 0)
    def _():
        pl.semaphore_wait(go, 1)

    arrived(wd.at[oc], core_rs.at[0])
    arrived(tgt_r, core_rs.at[1])
    base = tgt[c] + tgt_r[...]
    for i in range(NC):
        for t in range(quarter):
            arrived(ht.at[i, t], a2_rs.at[i * quarter + t])

    part = -base
    for i in range(NC):
        part = part + nn(ht[i].reshape(half, ht.shape[-1])[:, :ff], wd[i])
    groups = half // 8
    for h in range(2):
        res_s[groups * h : groups * h + groups] = part[:, cols * h : cols * h + cols].reshape(groups, 8, cols)
    sent_b = []
    for j, (dz, dy) in enumerate(WINDOW):
        zz, yy = at(dz, dy)
        sent_b.append(send(res_s.at[owned(zz, yy)], res_r.at[j], b1_ss.at[j], b1_rs.at[j], device(zz, yy, c, mp)))
    sent.append(send(ht.at[oc], ht2, core_ss.at[2], core_rs.at[2], partner))
    left(sent)

    @pl.when(own_half != c)
    def _():
        give.wait_send()

    mine = owned(z, y)
    total = res_s[mine]
    for j in reversed(range(len(WINDOW))):
        arrived(res_r.at[j], b1_rs.at[j])
        total = total + res_r[j]
    win[...] = total
    for j, (dz, dy) in enumerate(FAR):
        zz, yy = at(dz, dy)
        sent_b.append(send(win, far_r.at[j], b2_ss.at[j], b2_rs.at[j], device(zz, yy, c, mp)))
    sent_act = []
    for d in MP_ORDER:
        mm = lax.rem(mp + d, NM)
        sent_act.append(send(act.at[mp], act.at[mp], act_ss.at[d], act_rs.at[mp], device(z, y, c, mm)))
    left(sent_b[: len(WINDOW)])
    residual = total
    for j in range(len(FAR)):
        arrived(far_r.at[j], b2_rs.at[j])
        residual = residual + far_r[j]
    piece[...] = (residual * (1.0 / math.sqrt(2 * half))).astype(BF16)
    sent = []
    for j, (dz, dy) in enumerate(WINDOW):
        zz, yy = at(dz, dy)
        sent.append(send(piece, dfull.at[c, mine], c_ss.at[j], c_rs.at[j], device(zz, yy, c, mp)))
    dfull[c, mine] = piece[...]
    left(sent_b[len(WINDOW) :])
    for j, (dz, dy) in enumerate(WINDOW):
        zz, yy = at(dz, dy, -1)
        arrived(dfull.at[c, owned(zz, yy)], c_rs.at[j])

    def d_half(i, h):
        return dfull[i, groups * h : groups * h + groups].reshape(half, cols)

    def packed(rows):
        low, high = rows[:, :128], rows[:, 128:]
        return jnp.concatenate([low, jnp.concatenate([high[: half // 2], high[half // 2 :]], axis=1)], axis=0)

    d_own = [d_half(c, h) for h in range(2)]
    sent_d = []
    for e in (1, 0):
        i = lax.rem(c + e, NC)
        part = packed(nt(d_own[0], wd[i, :, :cols]) + nt(d_own[1], wd[i, :, cols:]))
        dh_s[e] = part.astype(BF16)
        dh_f[e] = part
        for d in MP_ORDER:
            mm = lax.rem(mp + d, NM)
            k = e * NM + d
            sent_d.append(send(dh_s.at[e], dh_r.at[c, mp], d1_ss.at[k], d1_rs.at[c * NM + mp], device(z, y, i, mm)))
        if e:
            sent_d.append(send(dh_f.at[e], dh_p, core_ss.at[4], core_rs.at[4], partner))
    sent.append(send(dfull.at[c], dfull.at[c], core_ss.at[3], core_rs.at[3], partner))
    left(sent)
    left(sent_act)

    arrived(dfull.at[oc], core_rs.at[3])
    arrived(ht2, core_rs.at[2])
    h_own = ht[c].reshape(half, ht.shape[-1])[:, :ff]
    h_other = ht2[...].reshape(half, ht.shape[-1])[:, :ff]
    for h in range(2):
        d_nat = [d_half(i, h) for i in range(NC)]
        gd[:, cols * h : cols * h + cols] = tn(h_own, d_half(c, h)) + tn(h_other, d_half(oc, h))
        gp[:, cols * h : cols * h + cols] = -(nn(th[:, :half], d_nat[0]) + nn(th[:, half:], d_nat[1]))
    for d in MP_ORDER:
        mm = lax.rem(mp + d, NM)
        arrived(act.at[mm], act_rs.at[mm])

    arrived(dh_p, core_rs.at[4])
    for e in range(NC):
        i = lax.rem(c + e, NC)
        total = dh_f[0] if e == 0 else dh_p[...]
        for d in reversed(MP_ORDER):
            mm = lax.rem(mp + d, NM)
            arrived(dh_r.at[i, mm], d1_rs.at[i * NM + mm])
            total = total + dh_r[i, mm].astype(F32)
        gate = act[pl.ds(i * quarter, quarter)].reshape(half, act.shape[-1])
        high = total[half:]
        high = jnp.concatenate([high[:, : ff - 128], high[:, ff - 128 :]], axis=0)
        dpt[i, :, :128] = (total[:half] * gate[:, :128]).astype(BF16)
        dpt[i, :, 128:ff] = (high * gate[:, 128:ff]).astype(BF16)
    left(sent_d)


def last_kernel(dpt, x, gd, gp, gu_h, gd_h, gp_h, gu, sem):
    ff = gu.shape[0]
    done = [pltpu.make_async_copy(gd, gd_h, sem.at[0]), pltpu.make_async_copy(gp, gp_h, sem.at[1])]
    for copy in done:
        copy.start()
    rows = dpt[...].reshape(x.shape[0], dpt.shape[-1])[:, :ff]
    step = x.shape[1] // 3
    for i in range(3):
        gu[:, step * i : step * i + step] = tn(rows, x[:, step * i : step * i + step])
        copy = pltpu.make_async_copy(
            gu.at[:, pl.ds(step * i, step)], gu_h.at[:, pl.ds(step * i, step)], sem.at[2 + i]
        )
        copy.start()
        done.append(copy)
    for copy in done:
        copy.wait()


def body(student_in, teacher_hidden, w_up, w_down, w_proj):
    tokens, width = student_in.shape
    ff, td = w_up.shape[0], w_proj.shape[0]
    half, cols = tokens // 2, width // 2
    wide, fold = 256, half * ff // 128
    hbm, vmem = pl.BlockSpec(memory_space=pltpu.HBM), pl.BlockSpec(memory_space=pltpu.VMEM)
    any_ = pl.BlockSpec(memory_space=pl.ANY)
    sem = pltpu.SemaphoreType.DMA
    vm = pltpu.VMEM
    scratch = [
        vm((td, tokens), BF16), vm((ff, width), BF16), vm((NC, ff, width), BF16),
        vm((td, width), BF16),
        vm((NM, 16, wide), F32), vm((NM, 16, wide), F32), vm((NM, 16, wide), F32), vm((16, wide), BF16),
        vm((NC, NM // 2, 16, wide), BF16), vm((NM // 2, 16, wide), BF16),
        vm((NC, half, width), F32), vm((half, width), F32),
        vm((16, 8, cols), F32), vm((15, 8, cols), F32), vm((8, cols), F32), vm((3, 8, cols), F32),
        vm((8, cols), BF16), vm((NC, 16, 8, cols), BF16),
        vm((NC, fold, 128), BF16), vm((NC, fold, 128), F32), vm((fold, 128), F32), vm((NC, NM, fold, 128), BF16),
        pltpu.SemaphoreType.REGULAR, sem((5,)), sem((5,)), sem((5,)),
        sem((8,)), sem((8,)), sem((8,)), sem((8,)), sem((15,)), sem((15,)), sem((3,)), sem((3,)),
        sem((15,)), sem((15,)), sem((16,)), sem((16,)), sem((8,)), sem((8,)),
    ]
    grads = [jax.ShapeDtypeStruct((rows, width), F32) for rows in (ff, ff, td)]
    x, dpt, gd, gp = pl.pallas_call(
        step_kernel,
        out_shape=(
            jax.ShapeDtypeStruct((tokens, width), BF16),
            jax.ShapeDtypeStruct((NC, half, wide), BF16),
            *grads[1:],
        ),
        in_specs=[hbm] * 5,
        out_specs=(vmem,) * 4,
        scratch_shapes=scratch,
        compiler_params=pltpu.CompilerParams(
            collective_id=0, has_side_effects=True, vmem_limit_bytes=40 * 1024 * 1024
        ),
        name="distill_step",
    )(*(pltpu.with_memory_space_constraint(a, pltpu.HBM) for a in (student_in, teacher_hidden, w_up, w_down, w_proj)))
    return pl.pallas_call(
        last_kernel,
        out_shape=tuple(grads),
        in_specs=[vmem, vmem, any_, any_],
        out_specs=(any_,) * 3,
        scratch_shapes=[vm((ff, width), F32), sem((5,))],
        compiler_params=pltpu.CompilerParams(vmem_limit_bytes=4 * 1024 * 1024),
        name="grad_up",
    )(dpt, x, gd, gp)


def solution(mesh):
    return jax.shard_map(
        body,
        mesh=mesh,
        in_specs=(P(None, "mp"), P("dp", None), P("dp", "mp"), P("dp", "mp"), P("dp", "mp")),
        out_specs=(P("dp", "mp"), P("dp", "mp"), P("dp", "mp")),
        check_vma=False,
    )
```

```python
import math

import jax
import jax.numpy as jnp
from jax import lax
from jax.experimental import pallas as pl
from jax.experimental.pallas import tpu as pltpu
from jax.sharding import PartitionSpec as P

F32, BF16 = jnp.float32, jnp.bfloat16
NZ, NY, NC, NX, NL = 16, 4, 2, 4, 2
NM = NX * NL
MESH = pl.DeviceIdType.MESH

WINDOW = (
    (0, 2), (2, 1), (2, -1), (3, 0), (-3, 0), (1, 1), (1, -1), (-1, 1), (-1, -1),
    (2, 0), (-2, 0), (0, 1), (0, -1), (1, 0), (-1, 0),
)
FAR = ((8, 0), (4, 2), (-4, 2))
MP_ORDER = (5, 3, 4, 2, 6, 7, 1)


def nt(a, b):
    return lax.dot_general(a, b, (((1,), (1,)), ((), ())), preferred_element_type=F32)


def tn(a, b):
    return lax.dot_general(a, b, (((0,), (0,)), ((), ())), preferred_element_type=F32)


def nn(a, b):
    return jnp.dot(a, b, preferred_element_type=F32)


def step_kernel(
    x_h, th_h, wu_h, wd_h, wp_h,
    x, dpt, gd, gp,
    th, wu, wd, wp,
    pre_s, pre_r, act, hid, ht, ht2, tgt, tgt_r,
    res_s, res_r, win, far_r, piece, dfull, dh_s, dh_f, dh_p, dh_r,
    go, in_sem, core_ss, core_rs,
    a1_ss, a1_rs, a2_ss, a2_rs, b1_ss, b1_rs, b2_ss, b2_rs, c_ss, c_rs, d1_ss, d1_rs, act_ss, act_rs,
):
    ff = wu.shape[0]
    half = x.shape[0] // 2
    cols = piece.shape[1]
    quarter = NM // 2
    dp, mp = lax.axis_index("dp"), lax.axis_index("mp")
    z, y, c = dp // (NY * NC), (dp // NC) % NY, dp % NC
    oc = 1 - c
    mirror = 1 - 2 * c
    own_half = mp // quarter
    tok = mp % quarter

    loads = [
        pltpu.make_async_copy(src, dst, in_sem.at[i])
        for i, (src, dst) in enumerate(((x_h, x), (wu_h, wu), (th_h, th), (wp_h, wp), (wd_h, wd.at[c])))
    ]
    loads[0].start()
    loads[1].start()

    def at(dz, dy, sign=1):
        return lax.rem(z + sign * mirror * dz + NZ, NZ), lax.rem(y + sign * dy + NY, NY)

    def device(zz, yy, cc, mm):
        return (zz * (NY * NC) + yy * NC + cc, mm)

    def owned(zz, yy):
        return lax.rem(yy + 2 * (zz // 4), NY) * 4 + lax.rem(zz, 4)

    def signal(sem, dev):
        pl.semaphore_signal(sem, inc=1, device_id=dev, device_id_type=MESH)

    partner = device(z, y, oc, mp)
    barrier = pltpu.get_barrier_semaphore()
    for d in MP_ORDER:
        signal(barrier, device(z, y, 0, lax.rem(mp + d, NM)))

    @pl.when(c == 1)
    def _():
        signal(barrier, partner)

    for dz, dy in FAR + WINDOW:
        zz, yy = at(dz, dy, -1)
        signal(barrier, device(zz, yy, 1, mp))
    for load in loads[2:]:
        load.start()

    def send(src, dst, ss, rs, dev):
        copy = pltpu.make_async_remote_copy(
            src_ref=src, dst_ref=dst, send_sem=ss, recv_sem=rs, device_id=dev, device_id_type=MESH
        )
        copy.start()
        return copy

    def arrived(dst, sem):
        pltpu.make_async_copy(dst, dst, sem).wait()

    def left(copies):
        for copy in copies:
            copy.wait_send()

    loads[0].wait()
    loads[1].wait()
    part = nt(x[...], wu[...])
    for m in range(NM):
        pre_s[m, :, :ff] = part[16 * m : 16 * m + 16]

    @pl.when(c == 0)
    def _():
        pl.semaphore_wait(barrier, NC * NM - 1)
        signal(go, partner)

    @pl.when(c == 1)
    def _():
        pl.semaphore_wait(go, 1)

    sent = []
    for d in MP_ORDER:
        mm = lax.rem(mp + d, NM)
        sent.append(send(pre_s.at[mm], pre_r.at[mp], a1_ss.at[d], a1_rs.at[mp], device(z, y, c, mm)))
    loads[4].wait()
    sent.append(send(wd.at[c], wd.at[c], core_ss.at[0], core_rs.at[0], partner))

    loads[2].wait()
    loads[3].wait()
    goal = tn(th[...], wp[...])
    for i in range(NC):
        tgt[i] = goal[half * i : half * i + half]
    sent.append(send(tgt.at[oc], tgt_r, core_ss.at[1], core_rs.at[1], partner))

    total = pre_s[mp]
    for d in reversed(MP_ORDER):
        mm = lax.rem(mp + d, NM)
        arrived(pre_r.at[mm], a1_rs.at[mm])
        total = total + pre_r[mm]
    active = jnp.maximum(total, 0.0)
    hid[...] = (active * active).astype(BF16)
    slot = c * quarter + tok
    for d in MP_ORDER:
        mm = lax.rem(mp + d, NM)
        sent.append(send(hid, ht.at[c, tok], a2_ss.at[d], a2_rs.at[slot], device(z, y, own_half, mm)))
    keep = pltpu.make_async_copy(hid, ht.at[c, tok], a2_rs.at[slot])
    give = pltpu.make_async_remote_copy(
        src_ref=hid, dst_ref=ht.at[c, tok], send_sem=a2_ss.at[0], recv_sem=a2_rs.at[slot],
        device_id=partner, device_id_type=MESH,
    )

    @pl.when(own_half == c)
    def _():
        keep.start()

    @pl.when(own_half != c)
    def _():
        give.start()

    act[mp] = 2.0 * active

    @pl.when(c == 1)
    def _():
        pl.semaphore_wait(barrier, NC * (len(FAR) + len(WINDOW)))
        signal(go, partner)

    @pl.when(c == 0)
    def _():
        pl.semaphore_wait(go, 1)

    arrived(wd.at[oc], core_rs.at[0])
    arrived(tgt_r, core_rs.at[1])
    base = tgt[c] + tgt_r[...]
    for i in range(NC):
        for t in range(quarter):
            arrived(ht.at[i, t], a2_rs.at[i * quarter + t])

    part = -base
    for i in range(NC):
        part = part + nn(ht[i].reshape(half, ht.shape[-1])[:, :ff], wd[i])
    groups = half // 8
    for h in range(2):
        res_s[groups * h : groups * h + groups] = part[:, cols * h : cols * h + cols].reshape(groups, 8, cols)
    sent_b = []
    for j, (dz, dy) in enumerate(WINDOW):
        zz, yy = at(dz, dy)
        sent_b.append(send(res_s.at[owned(zz, yy)], res_r.at[j], b1_ss.at[j], b1_rs.at[j], device(zz, yy, c, mp)))
    sent.append(send(ht.at[oc], ht2, core_ss.at[2], core_rs.at[2], partner))
    left(sent)

    @pl.when(own_half != c)
    def _():
        give.wait_send()

    mine = owned(z, y)
    total = res_s[mine]
    for j in reversed(range(len(WINDOW))):
        arrived(res_r.at[j], b1_rs.at[j])
        total = total + res_r[j]
    win[...] = total
    for j, (dz, dy) in enumerate(FAR):
        zz, yy = at(dz, dy)
        sent_b.append(send(win, far_r.at[j], b2_ss.at[j], b2_rs.at[j], device(zz, yy, c, mp)))
    sent_act = []
    for d in MP_ORDER:
        mm = lax.rem(mp + d, NM)
        sent_act.append(send(act.at[mp], act.at[mp], act_ss.at[d], act_rs.at[mp], device(z, y, c, mm)))
    left(sent_b[: len(WINDOW)])
    residual = total
    for j in range(len(FAR)):
        arrived(far_r.at[j], b2_rs.at[j])
        residual = residual + far_r[j]
    piece[...] = (residual * (1.0 / math.sqrt(2 * half))).astype(BF16)
    sent = []
    for j, (dz, dy) in enumerate(WINDOW):
        zz, yy = at(dz, dy)
        sent.append(send(piece, dfull.at[c, mine], c_ss.at[j], c_rs.at[j], device(zz, yy, c, mp)))
    dfull[c, mine] = piece[...]
    left(sent_b[len(WINDOW) :])
    for j, (dz, dy) in enumerate(WINDOW):
        zz, yy = at(dz, dy, -1)
        arrived(dfull.at[c, owned(zz, yy)], c_rs.at[j])

    def d_half(i, h):
        return dfull[i, groups * h : groups * h + groups].reshape(half, cols)

    def packed(rows):
        low, high = rows[:, :128], rows[:, 128:]
        return jnp.concatenate([low, jnp.concatenate([high[: half // 2], high[half // 2 :]], axis=1)], axis=0)

    d_own = [d_half(c, h) for h in range(2)]
    sent_d = []
    for i in (1, 0):
        part = packed(nt(d_own[0], wd[i, :, :cols]) + nt(d_own[1], wd[i, :, cols:]))
        dh_s[i] = part.astype(BF16)
        dh_f[i] = part
        for k in range(NM - 1):
            mm = k + jnp.where(k >= mp, 1, 0)
            ss = d1_ss.at[i * NM + k]
            sent_d.append(send(dh_s.at[i], dh_r.at[c, mp], ss, d1_rs.at[c * NM + mp], device(z, y, i, mm)))
    sent_d.append(send(dh_f.at[oc], dh_p, core_ss.at[4], core_rs.at[4], partner))
    sent.append(send(dfull.at[c], dfull.at[c], core_ss.at[3], core_rs.at[3], partner))
    left(sent)
    left(sent_act)

    arrived(dfull.at[oc], core_rs.at[3])
    arrived(ht2, core_rs.at[2])
    h_own = ht[c].reshape(half, ht.shape[-1])[:, :ff]
    h_other = ht2[...].reshape(half, ht.shape[-1])[:, :ff]
    for h in range(2):
        d_nat = [d_half(i, h) for i in range(NC)]
        gd[:, cols * h : cols * h + cols] = tn(h_own, d_half(c, h)) + tn(h_other, d_half(oc, h))
        gp[:, cols * h : cols * h + cols] = -(nn(th[:, :half], d_nat[0]) + nn(th[:, half:], d_nat[1]))
    for d in MP_ORDER:
        mm = lax.rem(mp + d, NM)
        arrived(act.at[mm], act_rs.at[mm])

    arrived(dh_p, core_rs.at[4])
    for e in range(NC):
        i = lax.rem(c + e, NC)
        total = dh_f[c] if e == 0 else dh_p[...]
        for k in range(NM - 1):
            mm = k + jnp.where(k >= mp, 1, 0)
            arrived(dh_r.at[i, mm], d1_rs.at[i * NM + mm])
            total = total + dh_r[i, mm].astype(F32)
        gate = act[pl.ds(i * quarter, quarter)].reshape(half, act.shape[-1])
        high = total[half:]
        high = jnp.concatenate([high[:, : ff - 128], high[:, ff - 128 :]], axis=0)
        dpt[i, :, :128] = (total[:half] * gate[:, :128]).astype(BF16)
        dpt[i, :, 128:ff] = (high * gate[:, 128:ff]).astype(BF16)
    left(sent_d)


def last_kernel(dpt, x, gd, gp, gu_h, gd_h, gp_h, gu, sem):
    ff = gu.shape[0]
    done = [pltpu.make_async_copy(gd, gd_h, sem.at[0]), pltpu.make_async_copy(gp, gp_h, sem.at[1])]
    for copy in done:
        copy.start()
    rows = dpt[...].reshape(x.shape[0], dpt.shape[-1])[:, :ff]
    step = x.shape[1] // 3
    for i in range(3):
        gu[:, step * i : step * i + step] = tn(rows, x[:, step * i : step * i + step])
        copy = pltpu.make_async_copy(
            gu.at[:, pl.ds(step * i, step)], gu_h.at[:, pl.ds(step * i, step)], sem.at[2 + i]
        )
        copy.start()
        done.append(copy)
    for copy in done:
        copy.wait()


def body(student_in, teacher_hidden, w_up, w_down, w_proj):
    tokens, width = student_in.shape
    ff, td = w_up.shape[0], w_proj.shape[0]
    half, cols = tokens // 2, width // 2
    wide, fold = 256, half * ff // 128
    hbm, vmem = pl.BlockSpec(memory_space=pltpu.HBM), pl.BlockSpec(memory_space=pltpu.VMEM)
    any_ = pl.BlockSpec(memory_space=pl.ANY)
    sem = pltpu.SemaphoreType.DMA
    vm = pltpu.VMEM
    scratch = [
        vm((td, tokens), BF16), vm((ff, width), BF16), vm((NC, ff, width), BF16),
        vm((td, width), BF16),
        vm((NM, 16, wide), F32), vm((NM, 16, wide), F32), vm((NM, 16, wide), F32), vm((16, wide), BF16),
        vm((NC, NM // 2, 16, wide), BF16), vm((NM // 2, 16, wide), BF16),
        vm((NC, half, width), F32), vm((half, width), F32),
        vm((16, 8, cols), F32), vm((15, 8, cols), F32), vm((8, cols), F32), vm((3, 8, cols), F32),
        vm((8, cols), BF16), vm((NC, 16, 8, cols), BF16),
        vm((NC, fold, 128), BF16), vm((NC, fold, 128), F32), vm((fold, 128), F32), vm((NC, NM, fold, 128), BF16),
        pltpu.SemaphoreType.REGULAR, sem((5,)), sem((5,)), sem((5,)),
        sem((8,)), sem((8,)), sem((8,)), sem((8,)), sem((15,)), sem((15,)), sem((3,)), sem((3,)),
        sem((15,)), sem((15,)), sem((16,)), sem((16,)), sem((8,)), sem((8,)),
    ]
    grads = [jax.ShapeDtypeStruct((rows, width), F32) for rows in (ff, ff, td)]
    x, dpt, gd, gp = pl.pallas_call(
        step_kernel,
        out_shape=(
            jax.ShapeDtypeStruct((tokens, width), BF16),
            jax.ShapeDtypeStruct((NC, half, wide), BF16),
            *grads[1:],
        ),
        in_specs=[hbm] * 5,
        out_specs=(vmem,) * 4,
        scratch_shapes=scratch,
        compiler_params=pltpu.CompilerParams(
            collective_id=0, has_side_effects=True, vmem_limit_bytes=40 * 1024 * 1024
        ),
        name="distill_step",
    )(*(pltpu.with_memory_space_constraint(a, pltpu.HBM) for a in (student_in, teacher_hidden, w_up, w_down, w_proj)))
    return pl.pallas_call(
        last_kernel,
        out_shape=tuple(grads),
        in_specs=[vmem, vmem, any_, any_],
        out_specs=(any_,) * 3,
        scratch_shapes=[vm((ff, width), F32), sem((5,))],
        compiler_params=pltpu.CompilerParams(vmem_limit_bytes=4 * 1024 * 1024),
        name="grad_up",
    )(dpt, x, gd, gp)


def solution(mesh):
    return jax.shard_map(
        body,
        mesh=mesh,
        in_specs=(P(None, "mp"), P("dp", None), P("dp", "mp"), P("dp", "mp"), P("dp", "mp")),
        out_specs=(P("dp", "mp"), P("dp", "mp"), P("dp", "mp")),
        check_vma=False,
    )
```

```python
import math

import jax
import jax.numpy as jnp
from jax import lax
from jax.experimental import pallas as pl
from jax.experimental.pallas import tpu as pltpu
from jax.sharding import PartitionSpec as P

F32, BF16 = jnp.float32, jnp.bfloat16
NZ, NY, NC, NX, NL = 16, 4, 2, 4, 2
NM = NX * NL
MESH = pl.DeviceIdType.MESH

WINDOW = (
    (0, 2), (2, 1), (2, -1), (3, 0), (-3, 0), (1, 1), (1, -1), (-1, 1), (-1, -1),
    (2, 0), (-2, 0), (0, 1), (0, -1), (1, 0), (-1, 0),
)
FAR = ((8, 0), (4, 2), (-4, 2))
MP_ORDER = (5, 3, 4, 2, 6, 7, 1)


def nt(a, b):
    return lax.dot_general(a, b, (((1,), (1,)), ((), ())), preferred_element_type=F32)


def tn(a, b):
    return lax.dot_general(a, b, (((0,), (0,)), ((), ())), preferred_element_type=F32)


def nn(a, b):
    return jnp.dot(a, b, preferred_element_type=F32)


def step_kernel(
    x_h, th_h, wu_h, wd_h, wp_h,
    x, dpt, gd, gp,
    th, wu, wd, wp,
    pre_s, pre_r, act, hid, ht, ht2, tgt, tgt_r,
    res_s, res_r, win, far_r, piece, dfull, dh_s, dh_f, dh_p, dh_r,
    go, in_sem, core_ss, core_rs,
    a1_ss, a1_rs, a2_ss, a2_rs, b1_ss, b1_rs, b2_ss, b2_rs, c_ss, c_rs, d1_ss, d1_rs, act_ss, act_rs,
):
    ff = wu.shape[0]
    half = x.shape[0] // 2
    cols = piece.shape[1]
    quarter = NM // 2
    dp, mp = lax.axis_index("dp"), lax.axis_index("mp")
    z, y, c = dp // (NY * NC), (dp // NC) % NY, dp % NC
    oc = 1 - c
    turn = 1 - 2 * (lax.rem(z, 4) // 2)
    own_half = mp // quarter
    tok = mp % quarter

    loads = [
        pltpu.make_async_copy(src, dst, in_sem.at[i])
        for i, (src, dst) in enumerate(((x_h, x), (wu_h, wu), (th_h, th), (wp_h, wp), (wd_h, wd.at[c])))
    ]
    loads[0].start()
    loads[1].start()

    def at(dz, dy, sign=1):
        step = turn * dz if dz == 2 and dy else sign * dz
        return lax.rem(z + step + NZ, NZ), lax.rem(y + sign * dy + NY, NY)

    def device(zz, yy, cc, mm):
        return (zz * (NY * NC) + yy * NC + cc, mm)

    def owned(zz, yy):
        return lax.rem(yy + 2 * (zz // 4), NY) * 4 + lax.rem(zz, 4)

    def signal(sem, dev):
        pl.semaphore_signal(sem, inc=1, device_id=dev, device_id_type=MESH)

    partner = device(z, y, oc, mp)
    barrier = pltpu.get_barrier_semaphore()
    for d in MP_ORDER:
        signal(barrier, device(z, y, 0, lax.rem(mp + d, NM)))

    @pl.when(c == 1)
    def _():
        signal(barrier, partner)

    for dz, dy in FAR + WINDOW:
        zz, yy = at(dz, dy, -1)
        signal(barrier, device(zz, yy, 1, mp))
    for load in loads[2:]:
        load.start()

    def send(src, dst, ss, rs, dev):
        copy = pltpu.make_async_remote_copy(
            src_ref=src, dst_ref=dst, send_sem=ss, recv_sem=rs, device_id=dev, device_id_type=MESH
        )
        copy.start()
        return copy

    def arrived(dst, sem):
        pltpu.make_async_copy(dst, dst, sem).wait()

    def left(copies):
        for copy in copies:
            copy.wait_send()

    loads[0].wait()
    loads[1].wait()
    part = nt(x[...], wu[...])
    for m in range(NM):
        pre_s[m, :, :ff] = part[16 * m : 16 * m + 16]

    @pl.when(c == 0)
    def _():
        pl.semaphore_wait(barrier, NC * NM - 1)
        signal(go, partner)

    @pl.when(c == 1)
    def _():
        pl.semaphore_wait(go, 1)

    sent = []
    for d in MP_ORDER:
        mm = lax.rem(mp + d, NM)
        sent.append(send(pre_s.at[mm], pre_r.at[mp], a1_ss.at[d], a1_rs.at[mp], device(z, y, c, mm)))
    loads[4].wait()
    sent.append(send(wd.at[c], wd.at[c], core_ss.at[0], core_rs.at[0], partner))

    loads[2].wait()
    loads[3].wait()
    goal = tn(th[...], wp[...])
    for i in range(NC):
        tgt[i] = goal[half * i : half * i + half]
    sent.append(send(tgt.at[oc], tgt_r, core_ss.at[1], core_rs.at[1], partner))

    total = pre_s[mp]
    for d in reversed(MP_ORDER):
        mm = lax.rem(mp + d, NM)
        arrived(pre_r.at[mm], a1_rs.at[mm])
        total = total + pre_r[mm]
    active = jnp.maximum(total, 0.0)
    hid[...] = (active * active).astype(BF16)
    slot = c * quarter + tok
    for d in MP_ORDER:
        mm = lax.rem(mp + d, NM)
        sent.append(send(hid, ht.at[c, tok], a2_ss.at[d], a2_rs.at[slot], device(z, y, own_half, mm)))
    keep = pltpu.make_async_copy(hid, ht.at[c, tok], a2_rs.at[slot])
    give = pltpu.make_async_remote_copy(
        src_ref=hid, dst_ref=ht.at[c, tok], send_sem=a2_ss.at[0], recv_sem=a2_rs.at[slot],
        device_id=partner, device_id_type=MESH,
    )

    @pl.when(own_half == c)
    def _():
        keep.start()

    @pl.when(own_half != c)
    def _():
        give.start()

    act[mp] = 2.0 * active

    @pl.when(c == 1)
    def _():
        pl.semaphore_wait(barrier, NC * (len(FAR) + len(WINDOW)))
        signal(go, partner)

    @pl.when(c == 0)
    def _():
        pl.semaphore_wait(go, 1)

    arrived(wd.at[oc], core_rs.at[0])
    arrived(tgt_r, core_rs.at[1])
    base = tgt[c] + tgt_r[...]
    for i in range(NC):
        for t in range(quarter):
            arrived(ht.at[i, t], a2_rs.at[i * quarter + t])

    part = -base
    for i in range(NC):
        part = part + nn(ht[i].reshape(half, ht.shape[-1])[:, :ff], wd[i])
    groups = half // 8
    for h in range(2):
        res_s[groups * h : groups * h + groups] = part[:, cols * h : cols * h + cols].reshape(groups, 8, cols)
    sent_b = []
    for j, (dz, dy) in enumerate(WINDOW):
        zz, yy = at(dz, dy)
        sent_b.append(send(res_s.at[owned(zz, yy)], res_r.at[j], b1_ss.at[j], b1_rs.at[j], device(zz, yy, c, mp)))
    sent.append(send(ht.at[oc], ht2, core_ss.at[2], core_rs.at[2], partner))
    left(sent)

    @pl.when(own_half != c)
    def _():
        give.wait_send()

    mine = owned(z, y)
    total = res_s[mine]
    for j in reversed(range(len(WINDOW))):
        arrived(res_r.at[j], b1_rs.at[j])
        total = total + res_r[j]
    win[...] = total
    for j, (dz, dy) in enumerate(FAR):
        zz, yy = at(dz, dy)
        sent_b.append(send(win, far_r.at[j], b2_ss.at[j], b2_rs.at[j], device(zz, yy, c, mp)))
    sent_act = []
    for d in MP_ORDER:
        mm = lax.rem(mp + d, NM)
        sent_act.append(send(act.at[mp], act.at[mp], act_ss.at[d], act_rs.at[mp], device(z, y, c, mm)))
    left(sent_b[: len(WINDOW)])
    residual = total
    for j in range(len(FAR)):
        arrived(far_r.at[j], b2_rs.at[j])
        residual = residual + far_r[j]
    piece[...] = (residual * (1.0 / math.sqrt(2 * half))).astype(BF16)
    sent = []
    for j, (dz, dy) in enumerate(WINDOW):
        zz, yy = at(dz, dy)
        sent.append(send(piece, dfull.at[c, mine], c_ss.at[j], c_rs.at[j], device(zz, yy, c, mp)))
    dfull[c, mine] = piece[...]
    left(sent_b[len(WINDOW) :])
    for j, (dz, dy) in enumerate(WINDOW):
        zz, yy = at(dz, dy, -1)
        arrived(dfull.at[c, owned(zz, yy)], c_rs.at[j])

    def d_half(i, h):
        return dfull[i, groups * h : groups * h + groups].reshape(half, cols)

    def packed(rows):
        low, high = rows[:, :128], rows[:, 128:]
        return jnp.concatenate([low, jnp.concatenate([high[: half // 2], high[half // 2 :]], axis=1)], axis=0)

    d_own = [d_half(c, h) for h in range(2)]
    sent_d = []
    for i in (1, 0):
        part = packed(nt(d_own[0], wd[i, :, :cols]) + nt(d_own[1], wd[i, :, cols:]))
        dh_s[i] = part.astype(BF16)
        dh_f[i] = part
        for k in range(NM - 1):
            mm = k + jnp.where(k >= mp, 1, 0)
            ss = d1_ss.at[i * NM + k]
            sent_d.append(send(dh_s.at[i], dh_r.at[c, mp], ss, d1_rs.at[c * NM + mp], device(z, y, i, mm)))
    sent_d.append(send(dh_f.at[oc], dh_p, core_ss.at[4], core_rs.at[4], partner))
    sent.append(send(dfull.at[c], dfull.at[c], core_ss.at[3], core_rs.at[3], partner))
    left(sent)
    left(sent_act)

    arrived(dfull.at[oc], core_rs.at[3])
    arrived(ht2, core_rs.at[2])
    h_own = ht[c].reshape(half, ht.shape[-1])[:, :ff]
    h_other = ht2[...].reshape(half, ht.shape[-1])[:, :ff]
    for h in range(2):
        d_nat = [d_half(i, h) for i in range(NC)]
        gd[:, cols * h : cols * h + cols] = tn(h_own, d_half(c, h)) + tn(h_other, d_half(oc, h))
        gp[:, cols * h : cols * h + cols] = -(nn(th[:, :half], d_nat[0]) + nn(th[:, half:], d_nat[1]))
    for d in MP_ORDER:
        mm = lax.rem(mp + d, NM)
        arrived(act.at[mm], act_rs.at[mm])

    arrived(dh_p, core_rs.at[4])
    for e in range(NC):
        i = lax.rem(c + e, NC)
        total = dh_f[c] if e == 0 else dh_p[...]
        for k in range(NM - 1):
            mm = k + jnp.where(k >= mp, 1, 0)
            arrived(dh_r.at[i, mm], d1_rs.at[i * NM + mm])
            total = total + dh_r[i, mm].astype(F32)
        gate = act[pl.ds(i * quarter, quarter)].reshape(half, act.shape[-1])
        high = total[half:]
        high = jnp.concatenate([high[:, : ff - 128], high[:, ff - 128 :]], axis=0)
        dpt[i, :, :128] = (total[:half] * gate[:, :128]).astype(BF16)
        dpt[i, :, 128:ff] = (high * gate[:, 128:ff]).astype(BF16)
    left(sent_d)


def last_kernel(dpt, x, gd, gp, gu_h, gd_h, gp_h, gu, sem):
    ff = gu.shape[0]
    done = [pltpu.make_async_copy(gd, gd_h, sem.at[0]), pltpu.make_async_copy(gp, gp_h, sem.at[1])]
    for copy in done:
        copy.start()
    rows = dpt[...].reshape(x.shape[0], dpt.shape[-1])[:, :ff]
    step = x.shape[1] // 3
    for i in range(3):
        gu[:, step * i : step * i + step] = tn(rows, x[:, step * i : step * i + step])
        copy = pltpu.make_async_copy(
            gu.at[:, pl.ds(step * i, step)], gu_h.at[:, pl.ds(step * i, step)], sem.at[2 + i]
        )
        copy.start()
        done.append(copy)
    for copy in done:
        copy.wait()


def body(student_in, teacher_hidden, w_up, w_down, w_proj):
    tokens, width = student_in.shape
    ff, td = w_up.shape[0], w_proj.shape[0]
    half, cols = tokens // 2, width // 2
    wide, fold = 256, half * ff // 128
    hbm, vmem = pl.BlockSpec(memory_space=pltpu.HBM), pl.BlockSpec(memory_space=pltpu.VMEM)
    any_ = pl.BlockSpec(memory_space=pl.ANY)
    sem = pltpu.SemaphoreType.DMA
    vm = pltpu.VMEM
    scratch = [
        vm((td, tokens), BF16), vm((ff, width), BF16), vm((NC, ff, width), BF16),
        vm((td, width), BF16),
        vm((NM, 16, wide), F32), vm((NM, 16, wide), F32), vm((NM, 16, wide), F32), vm((16, wide), BF16),
        vm((NC, NM // 2, 16, wide), BF16), vm((NM // 2, 16, wide), BF16),
        vm((NC, half, width), F32), vm((half, width), F32),
        vm((16, 8, cols), F32), vm((15, 8, cols), F32), vm((8, cols), F32), vm((3, 8, cols), F32),
        vm((8, cols), BF16), vm((NC, 16, 8, cols), BF16),
        vm((NC, fold, 128), BF16), vm((NC, fold, 128), F32), vm((fold, 128), F32), vm((NC, NM, fold, 128), BF16),
        pltpu.SemaphoreType.REGULAR, sem((5,)), sem((5,)), sem((5,)),
        sem((8,)), sem((8,)), sem((8,)), sem((8,)), sem((15,)), sem((15,)), sem((3,)), sem((3,)),
        sem((15,)), sem((15,)), sem((16,)), sem((16,)), sem((8,)), sem((8,)),
    ]
    grads = [jax.ShapeDtypeStruct((rows, width), F32) for rows in (ff, ff, td)]
    x, dpt, gd, gp = pl.pallas_call(
        step_kernel,
        out_shape=(
            jax.ShapeDtypeStruct((tokens, width), BF16),
            jax.ShapeDtypeStruct((NC, half, wide), BF16),
            *grads[1:],
        ),
        in_specs=[hbm] * 5,
        out_specs=(vmem,) * 4,
        scratch_shapes=scratch,
        compiler_params=pltpu.CompilerParams(
            collective_id=0, has_side_effects=True, vmem_limit_bytes=40 * 1024 * 1024
        ),
        name="distill_step",
    )(*(pltpu.with_memory_space_constraint(a, pltpu.HBM) for a in (student_in, teacher_hidden, w_up, w_down, w_proj)))
    return pl.pallas_call(
        last_kernel,
        out_shape=tuple(grads),
        in_specs=[vmem, vmem, any_, any_],
        out_specs=(any_,) * 3,
        scratch_shapes=[vm((ff, width), F32), sem((5,))],
        compiler_params=pltpu.CompilerParams(vmem_limit_bytes=4 * 1024 * 1024),
        name="grad_up",
    )(dpt, x, gd, gp)


def solution(mesh):
    return jax.shard_map(
        body,
        mesh=mesh,
        in_specs=(P(None, "mp"), P("dp", None), P("dp", "mp"), P("dp", "mp"), P("dp", "mp")),
        out_specs=(P("dp", "mp"), P("dp", "mp"), P("dp", "mp")),
        check_vma=False,
    )
```

```python
import math

import jax
import jax.numpy as jnp
from jax import lax
from jax.experimental import pallas as pl
from jax.experimental.pallas import tpu as pltpu
from jax.sharding import PartitionSpec as P

F32, BF16 = jnp.float32, jnp.bfloat16
NZ, NY, NC, NX, NL = 16, 4, 2, 4, 2
NM = NX * NL
MESH = pl.DeviceIdType.MESH

WINDOW = (
    (1, 1), (1, -1), (-1, 1), (-1, -1), (0, 2), (2, 1), (2, -1), (3, 0), (-3, 0),
    (2, 0), (-2, 0), (0, 1), (0, -1), (1, 0), (-1, 0),
)
FAR = ((8, 0), (4, 2), (-4, 2))
MP_ORDER = (5, 3, 4, 2, 6, 7, 1)


def nt(a, b):
    return lax.dot_general(a, b, (((1,), (1,)), ((), ())), preferred_element_type=F32)


def tn(a, b):
    return lax.dot_general(a, b, (((0,), (0,)), ((), ())), preferred_element_type=F32)


def nn(a, b):
    return jnp.dot(a, b, preferred_element_type=F32)


def step_kernel(
    x_h, th_h, wu_h, wd_h, wp_h,
    x, dpt, gd, gp,
    th, wu, wd, wp,
    pre_s, pre_r, act, hid, ht, ht2, tgt, tgt_r,
    res_s, res_r, win, far_r, piece, dfull, dh_s, dh_f, dh_p, dh_r,
    go, in_sem, core_ss, core_rs,
    a1_ss, a1_rs, a2_ss, a2_rs, b1_ss, b1_rs, b2_ss, b2_rs, c_ss, c_rs, d1_ss, d1_rs, act_ss, act_rs,
):
    ff = wu.shape[0]
    half = x.shape[0] // 2
    cols = piece.shape[1]
    quarter = NM // 2
    dp, mp = lax.axis_index("dp"), lax.axis_index("mp")
    z, y, c = dp // (NY * NC), (dp // NC) % NY, dp % NC
    oc = 1 - c
    turn = 1 - 2 * (lax.rem(z, 4) // 2)
    own_half = mp // quarter
    tok = mp % quarter

    loads = [
        pltpu.make_async_copy(src, dst, in_sem.at[i])
        for i, (src, dst) in enumerate(((x_h, x), (wu_h, wu), (th_h, th), (wp_h, wp), (wd_h, wd.at[c])))
    ]
    loads[0].start()
    loads[1].start()

    def at(dz, dy, sign=1):
        step = turn * dz if dz == 2 and dy else sign * dz
        return lax.rem(z + step + NZ, NZ), lax.rem(y + sign * dy + NY, NY)

    def device(zz, yy, cc, mm):
        return (zz * (NY * NC) + yy * NC + cc, mm)

    def owned(zz, yy):
        return lax.rem(yy + 2 * (zz // 4), NY) * 4 + lax.rem(zz, 4)

    def signal(sem, dev):
        pl.semaphore_signal(sem, inc=1, device_id=dev, device_id_type=MESH)

    partner = device(z, y, oc, mp)
    barrier = pltpu.get_barrier_semaphore()
    for d in MP_ORDER:
        signal(barrier, device(z, y, 0, lax.rem(mp + d, NM)))

    @pl.when(c == 1)
    def _():
        signal(barrier, partner)

    for dz, dy in FAR + WINDOW:
        zz, yy = at(dz, dy, -1)
        signal(barrier, device(zz, yy, 1, mp))
    for load in loads[2:]:
        load.start()

    def send(src, dst, ss, rs, dev):
        copy = pltpu.make_async_remote_copy(
            src_ref=src, dst_ref=dst, send_sem=ss, recv_sem=rs, device_id=dev, device_id_type=MESH
        )
        copy.start()
        return copy

    def arrived(dst, sem):
        pltpu.make_async_copy(dst, dst, sem).wait()

    def left(copies):
        for copy in copies:
            copy.wait_send()

    loads[0].wait()
    loads[1].wait()
    part = nt(x[...], wu[...])
    for m in range(NM):
        pre_s[m, :, :ff] = part[16 * m : 16 * m + 16]

    @pl.when(c == 0)
    def _():
        pl.semaphore_wait(barrier, NC * NM - 1)
        signal(go, partner)

    @pl.when(c == 1)
    def _():
        pl.semaphore_wait(go, 1)

    sent = []
    for d in MP_ORDER:
        mm = lax.rem(mp + d, NM)
        sent.append(send(pre_s.at[mm], pre_r.at[mp], a1_ss.at[d], a1_rs.at[mp], device(z, y, c, mm)))
    loads[4].wait()
    sent.append(send(wd.at[c], wd.at[c], core_ss.at[0], core_rs.at[0], partner))

    loads[2].wait()
    loads[3].wait()
    goal = tn(th[...], wp[...])
    for i in range(NC):
        tgt[i] = goal[half * i : half * i + half]
    sent.append(send(tgt.at[oc], tgt_r, core_ss.at[1], core_rs.at[1], partner))

    total = pre_s[mp]
    for d in reversed(MP_ORDER):
        mm = lax.rem(mp + d, NM)
        arrived(pre_r.at[mm], a1_rs.at[mm])
        total = total + pre_r[mm]
    active = jnp.maximum(total, 0.0)
    hid[...] = (active * active).astype(BF16)
    slot = c * quarter + tok
    for d in MP_ORDER:
        mm = lax.rem(mp + d, NM)
        sent.append(send(hid, ht.at[c, tok], a2_ss.at[d], a2_rs.at[slot], device(z, y, own_half, mm)))
    keep = pltpu.make_async_copy(hid, ht.at[c, tok], a2_rs.at[slot])
    give = pltpu.make_async_remote_copy(
        src_ref=hid, dst_ref=ht.at[c, tok], send_sem=a2_ss.at[0], recv_sem=a2_rs.at[slot],
        device_id=partner, device_id_type=MESH,
    )

    @pl.when(own_half == c)
    def _():
        keep.start()

    @pl.when(own_half != c)
    def _():
        give.start()

    act[mp] = 2.0 * active

    @pl.when(c == 1)
    def _():
        pl.semaphore_wait(barrier, NC * (len(FAR) + len(WINDOW)))
        signal(go, partner)

    @pl.when(c == 0)
    def _():
        pl.semaphore_wait(go, 1)

    arrived(wd.at[oc], core_rs.at[0])
    arrived(tgt_r, core_rs.at[1])
    base = tgt[c] + tgt_r[...]
    for i in range(NC):
        for t in range(quarter):
            arrived(ht.at[i, t], a2_rs.at[i * quarter + t])

    part = -base
    for i in range(NC):
        part = part + nn(ht[i].reshape(half, ht.shape[-1])[:, :ff], wd[i])
    groups = half // 8
    for h in range(2):
        res_s[groups * h : groups * h + groups] = part[:, cols * h : cols * h + cols].reshape(groups, 8, cols)
    sent_b = []
    for j, (dz, dy) in enumerate(WINDOW):
        zz, yy = at(dz, dy)
        sent_b.append(send(res_s.at[owned(zz, yy)], res_r.at[j], b1_ss.at[j], b1_rs.at[j], device(zz, yy, c, mp)))
    sent.append(send(ht.at[oc], ht2, core_ss.at[2], core_rs.at[2], partner))
    left(sent)

    @pl.when(own_half != c)
    def _():
        give.wait_send()

    mine = owned(z, y)
    total = res_s[mine]
    for j in reversed(range(len(WINDOW))):
        arrived(res_r.at[j], b1_rs.at[j])
        total = total + res_r[j]
    win[...] = total
    for j, (dz, dy) in enumerate(FAR):
        zz, yy = at(dz, dy)
        sent_b.append(send(win, far_r.at[j], b2_ss.at[j], b2_rs.at[j], device(zz, yy, c, mp)))
    sent_act = []
    for d in MP_ORDER:
        mm = lax.rem(mp + d, NM)
        sent_act.append(send(act.at[mp], act.at[mp], act_ss.at[d], act_rs.at[mp], device(z, y, c, mm)))
    left(sent_b[: len(WINDOW)])
    residual = total
    for j in range(len(FAR)):
        arrived(far_r.at[j], b2_rs.at[j])
        residual = residual + far_r[j]
    piece[...] = (residual * (1.0 / math.sqrt(2 * half))).astype(BF16)
    sent = []
    for j, (dz, dy) in enumerate(WINDOW):
        zz, yy = at(dz, dy)
        sent.append(send(piece, dfull.at[c, mine], c_ss.at[j], c_rs.at[j], device(zz, yy, c, mp)))
    dfull[c, mine] = piece[...]
    left(sent_b[len(WINDOW) :])
    for j, (dz, dy) in enumerate(WINDOW):
        zz, yy = at(dz, dy, -1)
        arrived(dfull.at[c, owned(zz, yy)], c_rs.at[j])

    def d_half(i, h):
        return dfull[i, groups * h : groups * h + groups].reshape(half, cols)

    def packed(rows):
        low, high = rows[:, :128], rows[:, 128:]
        return jnp.concatenate([low, jnp.concatenate([high[: half // 2], high[half // 2 :]], axis=1)], axis=0)

    d_own = [d_half(c, h) for h in range(2)]
    sent_d = []
    for i in (1, 0):
        part = packed(nt(d_own[0], wd[i, :, :cols]) + nt(d_own[1], wd[i, :, cols:]))
        dh_s[i] = part.astype(BF16)
        dh_f[i] = part
        for k in range(NM - 1):
            mm = k + jnp.where(k >= mp, 1, 0)
            ss = d1_ss.at[i * NM + k]
            sent_d.append(send(dh_s.at[i], dh_r.at[c, mp], ss, d1_rs.at[c * NM + mp], device(z, y, i, mm)))
    sent_d.append(send(dh_f.at[oc], dh_p, core_ss.at[4], core_rs.at[4], partner))
    sent.append(send(dfull.at[c], dfull.at[c], core_ss.at[3], core_rs.at[3], partner))
    left(sent)
    left(sent_act)

    arrived(dfull.at[oc], core_rs.at[3])
    arrived(ht2, core_rs.at[2])
    h_own = ht[c].reshape(half, ht.shape[-1])[:, :ff]
    h_other = ht2[...].reshape(half, ht.shape[-1])[:, :ff]
    for h in range(2):
        d_nat = [d_half(i, h) for i in range(NC)]
        gd[:, cols * h : cols * h + cols] = tn(h_own, d_half(c, h)) + tn(h_other, d_half(oc, h))
        gp[:, cols * h : cols * h + cols] = -(nn(th[:, :half], d_nat[0]) + nn(th[:, half:], d_nat[1]))
    for d in MP_ORDER:
        mm = lax.rem(mp + d, NM)
        arrived(act.at[mm], act_rs.at[mm])

    arrived(dh_p, core_rs.at[4])
    for e in range(NC):
        i = lax.rem(c + e, NC)
        total = dh_f[c] if e == 0 else dh_p[...]
        for k in range(NM - 1):
            mm = k + jnp.where(k >= mp, 1, 0)
            arrived(dh_r.at[i, mm], d1_rs.at[i * NM + mm])
            total = total + dh_r[i, mm].astype(F32)
        gate = act[pl.ds(i * quarter, quarter)].reshape(half, act.shape[-1])
        high = total[half:]
        high = jnp.concatenate([high[:, : ff - 128], high[:, ff - 128 :]], axis=0)
        dpt[i, :, :128] = (total[:half] * gate[:, :128]).astype(BF16)
        dpt[i, :, 128:ff] = (high * gate[:, 128:ff]).astype(BF16)
    left(sent_d)


def last_kernel(dpt, x, gd, gp, gu_h, gd_h, gp_h, gu, sem):
    ff = gu.shape[0]
    done = [pltpu.make_async_copy(gd, gd_h, sem.at[0]), pltpu.make_async_copy(gp, gp_h, sem.at[1])]
    for copy in done:
        copy.start()
    rows = dpt[...].reshape(x.shape[0], dpt.shape[-1])[:, :ff]
    step = x.shape[1] // 3
    for i in range(3):
        gu[:, step * i : step * i + step] = tn(rows, x[:, step * i : step * i + step])
        copy = pltpu.make_async_copy(
            gu.at[:, pl.ds(step * i, step)], gu_h.at[:, pl.ds(step * i, step)], sem.at[2 + i]
        )
        copy.start()
        done.append(copy)
    for copy in done:
        copy.wait()


def body(student_in, teacher_hidden, w_up, w_down, w_proj):
    tokens, width = student_in.shape
    ff, td = w_up.shape[0], w_proj.shape[0]
    half, cols = tokens // 2, width // 2
    wide, fold = 256, half * ff // 128
    hbm, vmem = pl.BlockSpec(memory_space=pltpu.HBM), pl.BlockSpec(memory_space=pltpu.VMEM)
    any_ = pl.BlockSpec(memory_space=pl.ANY)
    sem = pltpu.SemaphoreType.DMA
    vm = pltpu.VMEM
    scratch = [
        vm((td, tokens), BF16), vm((ff, width), BF16), vm((NC, ff, width), BF16),
        vm((td, width), BF16),
        vm((NM, 16, wide), F32), vm((NM, 16, wide), F32), vm((NM, 16, wide), F32), vm((16, wide), BF16),
        vm((NC, NM // 2, 16, wide), BF16), vm((NM // 2, 16, wide), BF16),
        vm((NC, half, width), F32), vm((half, width), F32),
        vm((16, 8, cols), F32), vm((15, 8, cols), F32), vm((8, cols), F32), vm((3, 8, cols), F32),
        vm((8, cols), BF16), vm((NC, 16, 8, cols), BF16),
        vm((NC, fold, 128), BF16), vm((NC, fold, 128), F32), vm((fold, 128), F32), vm((NC, NM, fold, 128), BF16),
        pltpu.SemaphoreType.REGULAR, sem((5,)), sem((5,)), sem((5,)),
        sem((8,)), sem((8,)), sem((8,)), sem((8,)), sem((15,)), sem((15,)), sem((3,)), sem((3,)),
        sem((15,)), sem((15,)), sem((16,)), sem((16,)), sem((8,)), sem((8,)),
    ]
    grads = [jax.ShapeDtypeStruct((rows, width), F32) for rows in (ff, ff, td)]
    x, dpt, gd, gp = pl.pallas_call(
        step_kernel,
        out_shape=(
            jax.ShapeDtypeStruct((tokens, width), BF16),
            jax.ShapeDtypeStruct((NC, half, wide), BF16),
            *grads[1:],
        ),
        in_specs=[hbm] * 5,
        out_specs=(vmem,) * 4,
        scratch_shapes=scratch,
        compiler_params=pltpu.CompilerParams(
            collective_id=0, has_side_effects=True, vmem_limit_bytes=40 * 1024 * 1024
        ),
        name="distill_step",
    )(*(pltpu.with_memory_space_constraint(a, pltpu.HBM) for a in (student_in, teacher_hidden, w_up, w_down, w_proj)))
    return pl.pallas_call(
        last_kernel,
        out_shape=tuple(grads),
        in_specs=[vmem, vmem, any_, any_],
        out_specs=(any_,) * 3,
        scratch_shapes=[vm((ff, width), F32), sem((5,))],
        compiler_params=pltpu.CompilerParams(vmem_limit_bytes=4 * 1024 * 1024),
        name="grad_up",
    )(dpt, x, gd, gp)


def solution(mesh):
    return jax.shard_map(
        body,
        mesh=mesh,
        in_specs=(P(None, "mp"), P("dp", None), P("dp", "mp"), P("dp", "mp"), P("dp", "mp")),
        out_specs=(P("dp", "mp"), P("dp", "mp"), P("dp", "mp")),
        check_vma=False,
    )
```
